32 devices in a mesh: groups: 2 (over x), dp: 16 (over z, y, core).
Axes of the slice: x: 2, y: 2, z: 4, core: 2. Of those that a mesh axis runs over, the one named last changes fastest.
Arguments:
- tokens: bfloat16 [4096, 8192], P(('groups', 'dp')), parts along dimension 0, may hold values from -6 to 6
- tenant: int32 [4096], P(('groups', 'dp')), parts along dimension 0, may hold values from 0 to 7
- plan: int32 [4096, 1], P(('groups', 'dp')), parts along dimension 0, may hold values from 0 to 15; in each aligned block of 128 rows (0 to 127, 128 to 255, ...) at most 16 rows name the same one
- frozen_key_weight: bfloat16 [8192, 512], P('dp'), may hold values from -0.0625 to 0.0625
- adapter_down_weight: bfloat16 [8192, 128], P('dp'), may hold values from -0.0625 to 0.0625
- adapter_up_weight: bfloat16 [128, 512], replicated, may hold values from -1.5 to 1.5
- cotangent: bfloat16 [8192, 512], P(('groups', 'dp')), parts along dimension 0, may hold values from -6 to 6
Outputs:
- placed_out: bfloat16 [8192, 512], P(('groups', 'dp')), parts along dimension 0
- token_gradient: bfloat16 [4096, 8192], P(('groups', 'dp')), parts along dimension 0
- down_grad: float32 [16384, 128], P(('groups', 'dp')), parts along dimension 0
- up_weight_gradient: float32 [256, 512], P('groups'), parts along dimension 0
The draws below stay inside these ranges and needn't reach their ends.
There are 2 independent parts, one for each index of `groups`. The reference program is written for one: setup_inputs(seed, part) draws one part's arguments, and reference() takes and returns one part's arrays. A program takes and returns all parts, laid end to end along the dimension named above; an argument that names none is the same for every part. Nothing has to cross between parts.
Inputs may be any that keep to these rules, and one draw needn't show every extreme that they name: `plan`: among the rows of one device, no device is named by more than 16 rows, and in every draw some device is named by exactly 16 rows of some device.
All inputs are finite; a program needn't handle non-finite values.
Results may differ from the reference program's by a relative error of at most 0.0047.
Values may be sent and summed in bfloat16 or wider, within the bound.
A program may use at most 64 MiB of HBM per device.

```python
import math
import jax
import jax.numpy as jnp
import numpy as np
from jax import lax

MODEL_WIDTH = 8192
KEY_FEATURES = 512
ADAPTER_RANK = 16
TENANT_COUNT = 8
TOK_DEV = 128
MOST = 16
TOKENS = 2048
ROUTED = 4096
N_DP = 16


def set_ends(entries, key, least, largest):
    dims = entries.shape
    spot = [jax.random.randint(jax.random.fold_in(key, axis), (), 0, dims[axis]) for axis in range(len(dims))]
    entries = entries.at[tuple(spot)].set(least)
    longest = dims.index(max(dims))
    spot[longest] = (spot[longest] + 1) % dims[longest]
    return entries.at[tuple(spot)].set(largest)


def shard_levels(own_key, shape, split, smallest, largest):
    factor_of, own = 1.0, jax.random.fold_in(own_key, 6)
    for dim, blocks in split:
        draws = jnp.exp(jax.random.uniform(jax.random.fold_in(own, dim), (blocks,), jnp.float32, smallest / len(split), largest / len(split)))
        factor_of = factor_of * jnp.repeat(draws, shape[dim] // blocks).reshape([-1 if axis == dim else 1 for axis in range(len(shape))])
    return factor_of


def rank_table(amount, slope):
    loads = [(1 << 20) // math.isqrt(standing ** slope) + 1 for standing in range(1, amount + 1)]
    width = 1 + sum(loads) // (1 << 30)
    return np.cumsum(np.array([max(1, weight // width) for weight in loads]))


def ranked(key, extent, count, lean):
    grid = rank_table(count, lean)
    pick = jax.random.randint(jax.random.fold_in(key, 1), extent, 0, int(grid[count - 1]))
    rank = jnp.searchsorted(jnp.asarray(grid, jnp.int32), pick, side="right")
    return jax.random.permutation(jax.random.fold_in(key, 2), count)[rank].astype(jnp.int32)


def deal_out(key, own, number, rows, number_of, top, bound, skew):
    ranking = jax.random.permutation(key, number_of)
    packed, ordinary = shares(number_of, rows * top, bound, skew, True), shares(number_of, rows * top, bound, skew, False)
    places = jnp.arange(number_of)

    def named(sizes, rotation):
        used = int((sizes > 0).sum())
        fixed = max(1, used // 4)
        passed = fixed + (places - fixed + rotation * (used - fixed)) % max(1, number_of - fixed)
        return jnp.zeros((number_of,), jnp.int32).at[ranking[jnp.where(places < fixed, places, passed)]].set(jnp.asarray(sizes, jnp.int32))

    sizes = jnp.where(number % 4 == 0, named(packed, number // 4), named(ordinary, number - number // 4 - 1))
    mixed = jax.random.permutation(jax.random.fold_in(own, 3), number_of)
    giver, receiver = mixed[0:number_of // 2 * 2:2], mixed[1:number_of // 2 * 2:2]
    room = jnp.minimum(sizes[giver] - 1, bound - sizes[receiver]) // 2
    room = jnp.where((giver == ranking[0]) | (receiver == ranking[0]) | (sizes[receiver] == 0), 0, jnp.maximum(room, 0))
    passed = jax.random.randint(jax.random.fold_in(own, 4), (number_of // 2,), 0, 1 << 20) % (room + 1)
    sizes = sizes.at[giver].add(-passed).at[receiver].add(passed)
    items = jnp.searchsorted(jnp.cumsum(sizes), jnp.arange(rows * top), side="right").astype(jnp.int32)
    table = items.reshape(top, rows).T
    table = table[jax.random.permutation(jax.random.fold_in(own, 1), rows)]
    rotation = jax.random.randint(jax.random.fold_in(own, 2), (rows, 1), 0, top)
    return jnp.take_along_axis(table, (jnp.arange(top)[None, :] + rotation) % top, axis=1)


def shares(amount, total, bound, skew, full):
    weights = [(1 << 20) // math.isqrt(grade ** skew) + 1 for grade in range(1, amount + 1)]
    largest = bound if full else min(bound, max(-(-total // amount), total * weights[0] // sum(weights)))
    least = 1 if total - largest >= amount - 1 else 0
    holding, surplus = [largest] + [least] * (amount - 1), total - largest - least * (amount - 1)
    while surplus > 0:
        free = [i for i in range(1, amount) if holding[i] < largest] or [i for i in range(1, amount) if holding[i] < bound]
        whole, remaining = sum([weights[i] for i in free]), surplus
        for i in free:
            addition = min(bound - holding[i], max(1, remaining * weights[i] // whole), surplus)
            holding[i] = holding[i] + addition
            surplus = surplus - addition
    return np.array(holding)


def scatter_about(rng, shape, spread, reach, shards=(), held_as=jnp.bfloat16):
    drawn = jax.random.normal(rng, shape, jnp.float32) * spread
    if len(shards) > 0:
        drawn = shard_levels(rng, shape, shards, -0.22, 0.18) * drawn
    return jnp.clip(drawn, min=-reach, max=reach).astype(held_as)


def setup_inputs(seed: int = 0, part: int = 0) -> dict:
    streams_of = jax.random.split(jax.random.key(seed), 8)
    part_splits = jax.random.split(jax.random.fold_in(streams_of[7], part), 8)
    tokens = scatter_about(part_splits[0], (TOKENS, MODEL_WIDTH), 1.0, 6.0, ((0, 16),))
    tenant = set_ends(ranked(part_splits[1], (TOKENS,), TENANT_COUNT, 2), jax.random.fold_in(part_splits[1], 3), 0, TENANT_COUNT - 1).astype(jnp.int32)
    plan_keys = jax.random.split(jax.random.fold_in(part_splits[2], 1), TOKENS // TOK_DEV)
    plan_turns = jax.random.permutation(jax.random.fold_in(part_splits[2], 3), TOKENS // TOK_DEV)
    plan = jax.vmap(lambda own, number: deal_out(jax.random.fold_in(part_splits[2], 2), own, number, TOK_DEV, N_DP, 1, MOST, 1))(plan_keys, plan_turns).reshape((TOKENS, 1))
    frozen_key_weight = scatter_about(streams_of[3], (MODEL_WIDTH, KEY_FEATURES), MODEL_WIDTH ** -0.5, 0.0625, ((0, 16),))
    adapter_down_weight = scatter_about(streams_of[4], (MODEL_WIDTH, TENANT_COUNT * ADAPTER_RANK), MODEL_WIDTH ** -0.5, 0.0625, ((0, 16),))
    adapter_up_weight = scatter_about(streams_of[5], (TENANT_COUNT * ADAPTER_RANK, KEY_FEATURES), ADAPTER_RANK ** -0.5, 1.5)
    cotangent = scatter_about(part_splits[6], (ROUTED, KEY_FEATURES), 1.0, 6.0, ((0, 16),))
    return dict(tokens=tokens, tenant=tenant, plan=plan, frozen_key_weight=frozen_key_weight, adapter_down_weight=adapter_down_weight, adapter_up_weight=adapter_up_weight, cotangent=cotangent)


adapter_scale = 2.0

def reference(tokens, tenant, plan, frozen_key_weight, adapter_down_weight, adapter_up_weight, cotangent):
    destination = plan[:, 0].reshape(N_DP, TOK_DEV)
    position = jnp.arange(TOK_DEV, dtype=jnp.int32)
    earlier_rows = (destination[:, None, :] == destination[:, :, None]) & (position[None, None, :] < position[None, :, None])
    rank_rows = lax.optimization_barrier(jnp.sum(earlier_rows.astype(jnp.int32), axis=2))
    source = jnp.arange(N_DP, dtype=jnp.int32)[:, None]
    slot_index = (destination * (N_DP * MOST) + source * MOST + rank_rows).reshape(-1).astype(jnp.int32)
    columns = jnp.arange(TENANT_COUNT * ADAPTER_RANK, dtype=jnp.int32) // ADAPTER_RANK
    tenant_picker = (columns[None, :] == tenant[:, None]).astype(jnp.float32)
    latent_state = (jnp.dot(tokens, adapter_down_weight, preferred_element_type=jnp.float32) * tenant_picker).astype(jnp.bfloat16)
    key_output = jnp.dot(tokens, frozen_key_weight, preferred_element_type=jnp.float32)
    key_output = (key_output + adapter_scale * jnp.dot(latent_state, adapter_up_weight, preferred_element_type=jnp.float32)).astype(jnp.bfloat16)
    placed_out = jnp.zeros((ROUTED, KEY_FEATURES), jnp.bfloat16).at[slot_index].set(key_output)
    row_gradient = cotangent[slot_index]
    mixing_factor = (adapter_scale * jnp.dot(row_gradient, adapter_up_weight.T, preferred_element_type=jnp.float32) * tenant_picker).astype(jnp.bfloat16)
    token_gradient = jnp.dot(row_gradient, frozen_key_weight.T, preferred_element_type=jnp.float32)
    token_gradient = (token_gradient + jnp.dot(mixing_factor, adapter_down_weight.T, preferred_element_type=jnp.float32)).astype(jnp.bfloat16)
    norm_multiplier = 1.0 / jnp.sqrt(jnp.float32(TOKENS))
    down_grad = jnp.dot(tokens.T, mixing_factor, preferred_element_type=jnp.float32) * norm_multiplier
    up_weight_gradient = adapter_scale * jnp.dot(latent_state.T, row_gradient, preferred_element_type=jnp.float32) * norm_multiplier
    return (placed_out, token_gradient, down_grad, up_weight_gradient)
```

```python
import functools

import jax
import jax.numpy as jnp
from jax import lax
from jax.experimental import pallas as pl
from jax.experimental.pallas import tpu as pltpu
from jax.sharding import PartitionSpec as P

ADAPTER_RANK = 16
SUBS = 2


adapter_scale = 2.0


def remote(src, dst, send_sem, recv_sem, target):
    return pltpu.make_async_remote_copy(
        src_ref=src,
        dst_ref=dst,
        send_sem=send_sem,
        recv_sem=recv_sem,
        device_id={"dp": target},
        device_id_type=pl.DeviceIdType.MESH,
    )


def greet_all(me, devices):
    barrier = pltpu.get_barrier_semaphore()
    for offset in range(1, devices):
        pl.semaphore_signal(
            barrier,
            inc=1,
            device_id={"dp": lax.rem(me + offset, devices)},
            device_id_type=pl.DeviceIdType.MESH,
        )
    pl.semaphore_wait(barrier, devices - 1)


def ring_position(chip, around):
    z, y = chip // 2, chip % 2
    return z + y * (around - 1 - 2 * z)


def ring_chip(position, around):
    back = position // (around // 2)
    return 2 * position + back * (2 * around - 1 - 4 * position)


def gather_kernel(
    devices, block_ref, cot_ref, full_ref, rows_ref,
    own_sem, own_cot_sem, ring_send, ring_recv, side_send, side_recv,
    own_side_send, own_side_recv, cot_send, cot_recv,
):
    me = lax.axis_index("dp")
    around = devices // 2
    chip, core = me // 2, me % 2
    sibling = chip * 2 + 1 - core
    spot = ring_position(chip, around)
    depth = block_ref.shape[0]
    piece = depth // (2 * SUBS)
    slots = cot_ref.shape[0] // devices

    def chip_at(hops):
        return ring_chip(lax.rem(spot + hops + around, around), around)

    def piece_of(device, way, sub):
        return full_ref.at[pl.ds(device * depth + (way * SUBS + sub) * piece, piece)]

    own = pltpu.make_async_copy(block_ref, full_ref.at[pl.ds(me * depth, depth)], own_sem)
    own.start()
    own_cot = pltpu.make_async_copy(
        cot_ref.at[pl.ds(me * slots, slots)], rows_ref.at[pl.ds(me * slots, slots)], own_cot_sem
    )
    own_cot.start()
    greet_all(me, devices)
    pending = []

    ways = (1, -1)
    for sub in range(SUBS):
        for way in range(2):
            source = block_ref.at[pl.ds((way * SUBS + sub) * piece, piece)]
            copy = remote(
                source, piece_of(me, way, sub), ring_send.at[way, sub, 0],
                ring_recv.at[way, sub, 0], chip_at(ways[way]) * 2 + core,
            )
            copy.start()
            pending.append(copy)
    side = remote(
        block_ref, full_ref.at[pl.ds(me * depth, depth)], own_side_send, own_side_recv, sibling
    )
    side.start()
    cots = []
    for offset in range(1, devices):
        peer = lax.rem(me + offset, devices)
        copy = remote(
            cot_ref.at[pl.ds(peer * slots, slots)], rows_ref.at[pl.ds(me * slots, slots)],
            cot_send.at[offset], cot_recv.at[offset], peer,
        )
        copy.start()
        cots.append(copy)

    sides = []
    for step in range(around - 1):
        for sub in range(SUBS):
            for way in range(2):
                origin = chip_at(-ways[way] * (step + 1))
                here = piece_of(origin * 2 + core, way, sub)
                remote(
                    here, here, ring_send.at[way, sub, step], ring_recv.at[way, sub, step], sibling
                ).wait_recv()
                if step < around - 2:
                    copy = remote(
                        here, here, ring_send.at[way, sub, step + 1],
                        ring_recv.at[way, sub, step + 1], chip_at(ways[way]) * 2 + core,
                    )
                    copy.start()
                    pending.append(copy)
                copy = remote(
                    here, here, side_send.at[way, sub, step], side_recv.at[way, sub, step], sibling
                )
                copy.start()
                sides.append((copy, piece_of(origin * 2 + 1 - core, way, sub), way, sub, step))

    own.wait()
    own_cot.wait()
    for offset in range(1, devices):
        cots[offset - 1].wait_send()
        origin = lax.rem(me - offset + devices, devices)
        place = rows_ref.at[pl.ds(origin * slots, slots)]
        remote(place, place, cot_send.at[offset], cot_recv.at[offset], sibling).wait_recv()
    for copy in pending:
        copy.wait_send()
    side.wait_send()
    place = full_ref.at[pl.ds(sibling * depth, depth)]
    remote(place, place, own_side_send, own_side_recv, sibling).wait_recv()
    for copy, place, way, sub, step in sides:
        copy.wait_send()
        remote(
            place, place, side_send.at[way, sub, step], side_recv.at[way, sub, step], sibling
        ).wait_recv()


def gather_blocks(devices, block, cotangent):
    dma = pltpu.SemaphoreType.DMA
    steps = devices // 2 - 1
    anywhere = pl.BlockSpec(memory_space=pl.ANY)
    return pl.pallas_call(
        functools.partial(gather_kernel, devices),
        out_shape=(
            jax.ShapeDtypeStruct((devices * block.shape[0], block.shape[1]), block.dtype),
            jax.ShapeDtypeStruct(cotangent.shape, cotangent.dtype),
        ),
        in_specs=[anywhere] * 2,
        out_specs=(anywhere, anywhere),
        scratch_shapes=[
            dma, dma,
            dma((2, SUBS, steps)), dma((2, SUBS, steps)),
            dma((2, SUBS, steps)), dma((2, SUBS, steps)),
            dma, dma,
            dma((devices,)), dma((devices,)),
        ],
        compiler_params=pltpu.CompilerParams(
            collective_id=0, has_side_effects=True, vmem_limit_bytes=48 * 1024 * 1024
        ),
    )(block, cotangent)


def finish_kernel(
    devices, scale, down_ref, up_ref, send_ref, down_out, up_out, placed_ref,
    side_buf, chip_buf, land_buf, up_buf, up_sum,
    own_sem, place_send, place_recv, up_send, up_recv, share_send, share_recv,
    side_send, side_recv, chip_send, chip_recv,
):
    me = lax.axis_index("dp")
    chips = devices // 2
    chip, core = me // 2, me % 2
    sibling = chip * 2 + 1 - core
    slots = send_ref.shape[0] // devices
    share = up_ref.shape[0] // devices

    own = pltpu.make_async_copy(
        send_ref.at[pl.ds(me * slots, slots)], placed_ref.at[pl.ds(me * slots, slots)], own_sem
    )
    own.start()
    greet_all(me, devices)

    sides = []
    for offset in list(range(1, chips)) + [0]:
        target = lax.rem(chip + offset, chips)
        copy = remote(
            down_ref.at[target * 2 + 1 - core], side_buf.at[offset],
            side_send.at[offset], side_recv.at[offset], sibling,
        )
        copy.start()
        sides.append(copy)
    ups, places = [], []
    for offset in range(1, devices):
        peer = lax.rem(me + offset, devices)
        copy = remote(
            up_ref.at[pl.ds(peer * share, share)], up_buf.at[offset],
            up_send.at[offset], up_recv.at[offset], peer,
        )
        copy.start()
        ups.append(copy)
    for offset in range(1, devices):
        peer = lax.rem(me + offset, devices)
        copy = remote(
            send_ref.at[pl.ds(peer * slots, slots)], placed_ref.at[pl.ds(me * slots, slots)],
            place_send.at[offset], place_recv.at[offset], peer,
        )
        copy.start()
        places.append(copy)

    sent = []
    for offset in range(1, chips):
        target = lax.rem(chip + offset, chips)
        sides[offset - 1].wait()
        chip_buf[offset] = (down_ref[target * 2 + core] + side_buf[offset]).astype(jnp.bfloat16)
        copy = remote(
            chip_buf.at[offset], land_buf.at[offset],
            chip_send.at[offset], chip_recv.at[offset], target * 2 + core,
        )
        copy.start()
        sent.append(copy)

    total = up_ref[pl.ds(pl.multiple_of(me * share, share), share), :]
    for offset in range(1, devices):
        ups[offset - 1].wait()
        total = total + up_buf[offset]
    up_sum[...] = total * scale
    up_out[pl.ds(pl.multiple_of(me * share, share), share), :] = total * scale
    shares = []
    for offset in range(1, devices):
        peer = lax.rem(me + offset, devices)
        copy = remote(
            up_sum, up_out.at[pl.ds(me * share, share)],
            share_send.at[offset], share_recv.at[offset], peer,
        )
        copy.start()
        shares.append(copy)

    sides[chips - 1].wait()
    down_out[...] = down_ref[me] + side_buf[0]
    for offset in range(1, chips):
        sent[offset - 1].wait()
        down_out[...] += land_buf[offset].astype(jnp.float32)
    down_out[...] *= scale

    own.wait()
    for offset in range(1, devices):
        origin = lax.rem(me - offset + devices, devices)
        places[offset - 1].wait_send()
        place = placed_ref.at[pl.ds(origin * slots, slots)]
        remote(place, place, place_send.at[offset], place_recv.at[offset], sibling).wait_recv()
        shares[offset - 1].wait_send()
        place = up_out.at[pl.ds(origin * share, share)]
        remote(place, place, share_send.at[offset], share_recv.at[offset], sibling).wait_recv()


def finish(devices, scale, down_part, up_portion, send_out):
    dma = pltpu.SemaphoreType.DMA
    chips = devices // 2
    depth, width = down_part.shape[0] // devices, down_part.shape[1]
    share, features = up_portion.shape[0] // devices, up_portion.shape[1]
    anywhere = pl.BlockSpec(memory_space=pl.ANY)
    local = pl.BlockSpec(memory_space=pltpu.VMEM)
    return pl.pallas_call(
        functools.partial(finish_kernel, devices, scale),
        out_shape=(
            jax.ShapeDtypeStruct((depth, width), jnp.float32),
            jax.ShapeDtypeStruct(up_portion.shape, jnp.float32),
            jax.ShapeDtypeStruct(send_out.shape, send_out.dtype),
        ),
        in_specs=[local, local, anywhere],
        out_specs=(local, local, anywhere),
        scratch_shapes=[
            pltpu.VMEM((chips, depth, width), jnp.float32),
            pltpu.VMEM((chips, depth, width), jnp.bfloat16),
            pltpu.VMEM((chips, depth, width), jnp.bfloat16),
            pltpu.VMEM((devices, share, features), jnp.float32),
            pltpu.VMEM((share, features), jnp.float32),
            dma,
            dma((devices,)), dma((devices,)),
            dma((devices,)), dma((devices,)),
            dma((devices,)), dma((devices,)),
            dma((chips,)), dma((chips,)),
            dma((chips,)), dma((chips,)),
        ],
        compiler_params=pltpu.CompilerParams(
            collective_id=1, has_side_effects=True, vmem_limit_bytes=48 * 1024 * 1024
        ),
    )(down_part.reshape(devices, depth, width), up_portion, send_out)


def place_rows(plan, slot_count, per_peer):
    destination = plan[:, 0]
    position = jnp.arange(destination.shape[0], dtype=jnp.int32)
    earlier_rows = (destination[None, :] == destination[:, None]) & (
        position[None, :] < position[:, None]
    )
    target_slot = destination * per_peer + jnp.sum(earlier_rows.astype(jnp.int32), axis=1)
    return (jnp.arange(slot_count, dtype=jnp.int32)[:, None] == target_slot[None, :]).astype(
        jnp.int32
    )


def tenant_mask(owners, feature_width):
    columns = jnp.arange(feature_width, dtype=jnp.int32) // ADAPTER_RANK
    return (columns[None, :] == owners[:, None]).astype(jnp.float32)


def leading_product(left, right):
    return lax.dot_general(
        left, right, (((0,), (0,)), ((), ())), preferred_element_type=jnp.float32
    )


def trailing_product(left, right):
    return lax.dot_general(
        left, right, (((1,), (1,)), ((), ())), preferred_element_type=jnp.float32
    )


def shards(
    tokens, tenant, plan, frozen_key_weight, adapter_down_weight, adapter_up_weight, cotangent
):
    devices = lax.axis_size("dp")
    slot_count = cotangent.shape[0]
    per_peer = slot_count // devices
    features = frozen_key_weight.shape[1]
    feature_width = adapter_down_weight.shape[1]
    direct = devices == 16
    block = jnp.concatenate([frozen_key_weight, adapter_down_weight], axis=1)
    if direct:
        complete, returned_cot = gather_blocks(devices, block, cotangent)
    else:
        complete = lax.all_gather(block, "dp", axis=0, tiled=True)
        returned_cot = lax.all_to_all(cotangent, "dp", split_axis=0, concat_axis=0, tiled=True)
    selector_rows = place_rows(plan, slot_count, per_peer).astype(jnp.bfloat16)
    tenant_picker = tenant_mask(tenant, feature_width)
    both = jnp.dot(tokens, complete, preferred_element_type=jnp.float32)
    latent_state = (both[:, features:] * tenant_picker).astype(jnp.bfloat16)
    key_output = (
        both[:, :features]
        + adapter_scale
        * jnp.dot(latent_state, adapter_up_weight, preferred_element_type=jnp.float32)
    ).astype(jnp.bfloat16)
    send_out = jnp.dot(selector_rows, key_output, preferred_element_type=jnp.float32).astype(
        jnp.bfloat16
    )
    row_gradient = leading_product(selector_rows, returned_cot).astype(jnp.bfloat16)
    mixing_factor = (
        adapter_scale * trailing_product(row_gradient, adapter_up_weight) * tenant_picker
    ).astype(jnp.bfloat16)
    token_gradient = trailing_product(
        jnp.concatenate([row_gradient, mixing_factor], axis=1), complete
    ).astype(jnp.bfloat16)
    scale = (tokens.shape[0] * devices) ** -0.5
    up_portion = adapter_scale * leading_product(latent_state, row_gradient)
    down_part = leading_product(tokens, mixing_factor)
    if direct:
        down_grad, up_weight_gradient, placed_out = finish(
            devices, scale, down_part, up_portion, send_out
        )
    else:
        placed_out = lax.all_to_all(send_out, "dp", split_axis=0, concat_axis=0, tiled=True)
        down_grad = lax.psum_scatter(down_part, "dp", scatter_dimension=0, tiled=True) * scale
        up_weight_gradient = lax.psum(up_portion, "dp") * scale
    return (placed_out, token_gradient, down_grad, up_weight_gradient)


def solution(mesh):
    return jax.shard_map(
        shards,
        mesh=mesh,
        in_specs=(
            P(("groups", "dp"), None),
            P(("groups", "dp")),
            P(("groups", "dp"), None),
            P("dp", None),
            P("dp", None),
            P(),
            P(("groups", "dp"), None),
        ),
        out_specs=(
            P(("groups", "dp"), None),
            P(("groups", "dp"), None),
            P(("groups", "dp"), None),
            P("groups", None),
        ),
        check_vma=False,
    )
```

```python
import functools

import jax
import jax.numpy as jnp
from jax import lax
from jax.experimental import pallas as pl
from jax.experimental.pallas import tpu as pltpu
from jax.sharding import PartitionSpec as P

ADAPTER_RANK = 16
SUBS = 2


adapter_scale = 2.0


def remote(src, dst, send_sem, recv_sem, target, axis="dp"):
    return pltpu.make_async_remote_copy(
        src_ref=src,
        dst_ref=dst,
        send_sem=send_sem,
        recv_sem=recv_sem,
        device_id={axis: target},
        device_id_type=pl.DeviceIdType.MESH,
    )


def greet_all(me, devices, twin=None):
    barrier = pltpu.get_barrier_semaphore()
    targets = [{"dp": lax.rem(me + offset, devices)} for offset in range(1, devices)]
    if twin is not None:
        targets.append({"groups": twin})
    for target in targets:
        pl.semaphore_signal(
            barrier, inc=1, device_id=target, device_id_type=pl.DeviceIdType.MESH
        )
    pl.semaphore_wait(barrier, len(targets))


def ring_position(chip, around):
    z, y = chip // 2, chip % 2
    return z + y * (around - 1 - 2 * z)


def ring_chip(position, around):
    back = position // (around // 2)
    return 2 * position + back * (2 * around - 1 - 4 * position)


def gather_kernel(
    devices, block_ref, cot_ref, full_ref, rows_ref,
    own_sem, own_cot_sem, ring_send, ring_recv, side_send, side_recv,
    own_side_send, own_side_recv, cot_send, cot_recv,
    twin_send, twin_recv, twin_side_send, twin_side_recv,
):
    me = lax.axis_index("dp")
    around = devices // 2
    chip, core = me // 2, me % 2
    sibling = chip * 2 + 1 - core
    spot = ring_position(chip, around)
    depth = block_ref.shape[0]
    group = lax.axis_index("groups")
    single = depth * 5 // 32
    double = depth // 2 - 2 * single
    slots = cot_ref.shape[0] // devices

    def chip_at(hops):
        return ring_chip(lax.rem(spot + hops + around, around), around)

    def rows_of(way, sub, holder):
        if sub == 0:
            return holder * (depth - 2 * single) + way * single, single
        return 2 * single + way * double, double

    def piece_of(device, way, sub, holder):
        first, count = rows_of(way, sub, holder)
        return full_ref.at[pl.ds(device * depth + first, count)]

    own = pltpu.make_async_copy(block_ref, full_ref.at[pl.ds(me * depth, depth)], own_sem)
    own.start()
    own_cot = pltpu.make_async_copy(
        cot_ref.at[pl.ds(me * slots, slots)], rows_ref.at[pl.ds(me * slots, slots)], own_cot_sem
    )
    own_cot.start()
    greet_all(me, devices, 1 - group)
    pending = []

    ways = (1, -1)
    for sub in range(SUBS):
        for way in range(2):
            first, count = rows_of(way, sub, group)
            copy = remote(
                block_ref.at[pl.ds(first, count)], piece_of(me, way, sub, group), ring_send.at[way, sub, 0],
                ring_recv.at[way, sub, 0], chip_at(ways[way]) * 2 + core,
            )
            copy.start()
            pending.append(copy)
    side = remote(
        block_ref, full_ref.at[pl.ds(me * depth, depth)], own_side_send, own_side_recv, sibling
    )
    side.start()
    cots = []
    for offset in range(1, devices):
        peer = lax.rem(me + offset, devices)
        copy = remote(
            cot_ref.at[pl.ds(peer * slots, slots)], rows_ref.at[pl.ds(me * slots, slots)],
            cot_send.at[offset], cot_recv.at[offset], peer,
        )
        copy.start()
        cots.append(copy)

    sides = []

    def relay_twin(step):
        for way in range(2):
            origin = chip_at(-ways[way] * (step + 1))
            here = piece_of(origin * 2 + core, way, 0, 1 - group)
            remote(
                here, here, twin_send.at[way, step], twin_recv.at[way, step], 1 - group, "groups"
            ).wait_recv()
            sems = twin_side_send.at[way, step], twin_side_recv.at[way, step]
            copy = remote(here, here, *sems, sibling)
            copy.start()
            sides.append((copy, piece_of(origin * 2 + 1 - core, way, 0, 1 - group), *sems))

    for step in range(around - 1):
        for sub in range(SUBS):
            for way in range(2):
                origin = chip_at(-ways[way] * (step + 1))
                here = piece_of(origin * 2 + core, way, sub, group)
                remote(
                    here, here, ring_send.at[way, sub, step], ring_recv.at[way, sub, step], sibling
                ).wait_recv()
                if step < around - 2:
                    copy = remote(
                        here, here, ring_send.at[way, sub, step + 1],
                        ring_recv.at[way, sub, step + 1], chip_at(ways[way]) * 2 + core,
                    )
                    copy.start()
                    pending.append(copy)
                if sub == 0:
                    copy = remote(
                        here, here, twin_send.at[way, step], twin_recv.at[way, step],
                        1 - group, "groups",
                    )
                    copy.start()
                    pending.append(copy)
                sems = side_send.at[way, sub, step], side_recv.at[way, sub, step]
                copy = remote(here, here, *sems, sibling)
                copy.start()
                sides.append((copy, piece_of(origin * 2 + 1 - core, way, sub, group), *sems))
        if step > 0:
            relay_twin(step - 1)
    relay_twin(around - 2)

    own.wait()
    own_cot.wait()
    for offset in range(1, devices):
        cots[offset - 1].wait_send()
        origin = lax.rem(me - offset + devices, devices)
        place = rows_ref.at[pl.ds(origin * slots, slots)]
        remote(place, place, cot_send.at[offset], cot_recv.at[offset], sibling).wait_recv()
    for copy in pending:
        copy.wait_send()
    side.wait_send()
    place = full_ref.at[pl.ds(sibling * depth, depth)]
    remote(place, place, own_side_send, own_side_recv, sibling).wait_recv()
    for copy, place, send_sem, recv_sem in sides:
        copy.wait_send()
        remote(place, place, send_sem, recv_sem, sibling).wait_recv()


def gather_blocks(devices, block, cotangent):
    dma = pltpu.SemaphoreType.DMA
    steps = devices // 2 - 1
    anywhere = pl.BlockSpec(memory_space=pl.ANY)
    return pl.pallas_call(
        functools.partial(gather_kernel, devices),
        out_shape=(
            jax.ShapeDtypeStruct((devices * block.shape[0], block.shape[1]), block.dtype),
            jax.ShapeDtypeStruct(cotangent.shape, cotangent.dtype),
        ),
        in_specs=[anywhere] * 2,
        out_specs=(anywhere, anywhere),
        scratch_shapes=[
            dma, dma,
            dma((2, SUBS, steps)), dma((2, SUBS, steps)),
            dma((2, SUBS, steps)), dma((2, SUBS, steps)),
            dma, dma,
            dma((devices,)), dma((devices,)),
            dma((2, steps)), dma((2, steps)),
            dma((2, steps)), dma((2, steps)),
        ],
        compiler_params=pltpu.CompilerParams(
            collective_id=0, has_side_effects=True, vmem_limit_bytes=48 * 1024 * 1024
        ),
    )(block, cotangent)


def finish_kernel(
    devices, scale, tokens_ref, mix_ref, up_ref, send_ref, down_out, up_out, placed_ref,
    part_buf, side_buf, y_buf, y_land, z_buf, z_land, up_side, up_buf, up_land,
    own_sem, place_send, place_recv, side_send, side_recv, y_send, y_recv, z_send, z_recv,
    up_side_send, up_side_recv, up_send, up_recv, share_send, share_recv, last_send, last_recv,
):
    me = lax.axis_index("dp")
    chips, deep = devices // 2, devices // 4
    chip, core = me // 2, me % 2
    z, y = chip // 2, chip % 2
    sibling = chip * 2 + 1 - core
    across = (z * 2 + 1 - y) * 2 + core
    slots = send_ref.shape[0] // devices
    depth = down_out.shape[0]
    order = list(range(1, deep)) + [0]

    def device_of(hop, row, parity):
        return (lax.rem(z + hop, deep) * 2 + row) * 2 + parity

    def part(device):
        columns = pl.ds(pl.multiple_of(device * depth, depth), depth)
        return leading_product(tokens_ref[:, columns], mix_ref[...])

    own = pltpu.make_async_copy(
        send_ref.at[pl.ds(me * slots, slots)], placed_ref.at[pl.ds(me * slots, slots)], own_sem
    )
    own.start()
    greet_all(me, devices)

    up_pair = remote(up_ref.at[:, 1 - core], up_side, up_side_send, up_side_recv, sibling)
    up_pair.start()
    places = []
    for offset in range(1, devices):
        peer = lax.rem(me + offset, devices)
        copy = remote(
            send_ref.at[pl.ds(peer * slots, slots)], placed_ref.at[pl.ds(me * slots, slots)],
            place_send.at[offset], place_recv.at[offset], peer,
        )
        copy.start()
        places.append(copy)

    sides = []
    for row in range(2):
        for hop in order:
            slot = row * deep + hop
            part_buf[slot] = part(device_of(hop, 1 - y if row == 0 else y, 1 - core))
            copy = remote(
                part_buf.at[slot], side_buf.at[slot], side_send.at[slot], side_recv.at[slot],
                sibling,
            )
            copy.start()
            sides.append(copy)
        if row == 0:
            over = []
            for hop in order:
                mine = part(device_of(hop, 1 - y, core))
                sides[len(over)].wait()
                y_buf[hop] = (mine + side_buf[hop]).astype(jnp.bfloat16)
                copy = remote(y_buf.at[hop], y_land.at[hop], y_send.at[hop], y_recv.at[hop], across)
                copy.start()
                over.append(copy)

    up_pair.wait()
    ups = []
    for offset in range(1, chips):
        target = lax.rem(chip + offset, chips)
        up_buf[offset] = up_ref[target, core] + up_side[target]
        copy = remote(
            up_buf.at[offset], up_land.at[offset], up_send.at[offset], up_recv.at[offset],
            target * 2 + core,
        )
        copy.start()
        ups.append(copy)

    along = []
    for count, hop in enumerate(order):
        mine = part(device_of(hop, y, core))
        sides[deep + count].wait()
        mine = mine + side_buf[deep + hop]
        over[count].wait()
        mine = mine + y_land[hop].astype(jnp.float32)
        if hop == 0:
            down_out[...] = mine
        else:
            z_buf[hop] = mine.astype(jnp.bfloat16)
            copy = remote(
                z_buf.at[hop], z_land.at[hop], z_send.at[hop], z_recv.at[hop],
                device_of(hop, y, core),
            )
            copy.start()
            along.append(copy)

    total = up_ref[chip, core] + up_side[chip]
    for offset in range(1, chips):
        ups[offset - 1].wait()
        total = total + up_land[offset]
    up_out[chip, core] = total * scale
    shares = []
    for offset in range(1, chips):
        target = lax.rem(chip + offset, chips)
        copy = remote(
            up_out.at[chip, core], up_out.at[chip, core],
            share_send.at[offset], share_recv.at[offset], target * 2 + core,
        )
        copy.start()
        shares.append(copy)
    for offset in range(1, chips):
        shares[offset - 1].wait_send()
        place = up_out.at[lax.rem(chip - offset + chips, chips), core]
        remote(place, place, share_send.at[offset], share_recv.at[offset], sibling).wait_recv()
    mine_up, other_up = up_out.at[:, core], up_out.at[:, 1 - core]
    last = remote(mine_up, mine_up, last_send, last_recv, sibling)
    last.start()

    for copy in along:
        copy.wait()
    total = down_out[...]
    for hop in range(1, deep):
        total = total + z_land[hop].astype(jnp.float32)
    down_out[...] = total * scale

    own.wait()
    for offset in range(1, devices):
        origin = lax.rem(me - offset + devices, devices)
        places[offset - 1].wait_send()
        place = placed_ref.at[pl.ds(origin * slots, slots)]
        remote(place, place, place_send.at[offset], place_recv.at[offset], sibling).wait_recv()
    last.wait_send()
    remote(other_up, other_up, last_send, last_recv, sibling).wait_recv()


def finish(devices, scale, tokens, mixing_factor, up_portion, send_out):
    dma = pltpu.SemaphoreType.DMA
    chips, deep = devices // 2, devices // 4
    depth, width = tokens.shape[1] // devices, mixing_factor.shape[1]
    share, features = up_portion.shape[0] // devices, up_portion.shape[1]
    anywhere = pl.BlockSpec(memory_space=pl.ANY)
    local = pl.BlockSpec(memory_space=pltpu.VMEM)
    up_shape = (chips, 2, share, features)
    down, up, placed = pl.pallas_call(
        functools.partial(finish_kernel, devices, scale),
        out_shape=(
            jax.ShapeDtypeStruct((depth, width), jnp.float32),
            jax.ShapeDtypeStruct(up_shape, jnp.float32),
            jax.ShapeDtypeStruct(send_out.shape, send_out.dtype),
        ),
        in_specs=[local, local, local, anywhere],
        out_specs=(local, local, anywhere),
        scratch_shapes=[
            pltpu.VMEM((chips, depth, width), jnp.float32),
            pltpu.VMEM((chips, depth, width), jnp.float32),
            pltpu.VMEM((deep, depth, width), jnp.bfloat16),
            pltpu.VMEM((deep, depth, width), jnp.bfloat16),
            pltpu.VMEM((deep, depth, width), jnp.bfloat16),
            pltpu.VMEM((deep, depth, width), jnp.bfloat16),
            pltpu.VMEM((chips, share, features), jnp.float32),
            pltpu.VMEM((chips, share, features), jnp.float32),
            pltpu.VMEM((chips, share, features), jnp.float32),
            dma,
            dma((devices,)), dma((devices,)),
            dma((chips,)), dma((chips,)),
            dma((deep,)), dma((deep,)),
            dma((deep,)), dma((deep,)),
            dma, dma,
            dma((chips,)), dma((chips,)),
            dma((chips,)), dma((chips,)),
            dma, dma,
        ],
        compiler_params=pltpu.CompilerParams(
            collective_id=1, has_side_effects=True, vmem_limit_bytes=48 * 1024 * 1024
        ),
    )(tokens, mixing_factor, up_portion.reshape(up_shape), send_out)
    return down, up.reshape(up_portion.shape), placed


def place_rows(plan, slot_count, per_peer):
    destination = plan[:, 0]
    position = jnp.arange(destination.shape[0], dtype=jnp.int32)
    earlier_rows = (destination[None, :] == destination[:, None]) & (
        position[None, :] < position[:, None]
    )
    target_slot = destination * per_peer + jnp.sum(earlier_rows.astype(jnp.int32), axis=1)
    return (jnp.arange(slot_count, dtype=jnp.int32)[:, None] == target_slot[None, :]).astype(
        jnp.int32
    )


def tenant_mask(owners, feature_width):
    columns = jnp.arange(feature_width, dtype=jnp.int32) // ADAPTER_RANK
    return (columns[None, :] == owners[:, None]).astype(jnp.float32)


def leading_product(left, right):
    return lax.dot_general(
        left, right, (((0,), (0,)), ((), ())), preferred_element_type=jnp.float32
    )


def trailing_product(left, right):
    return lax.dot_general(
        left, right, (((1,), (1,)), ((), ())), preferred_element_type=jnp.float32
    )


def shards(
    tokens, tenant, plan, frozen_key_weight, adapter_down_weight, adapter_up_weight, cotangent
):
    devices = lax.axis_size("dp")
    slot_count = cotangent.shape[0]
    per_peer = slot_count // devices
    features = frozen_key_weight.shape[1]
    feature_width = adapter_down_weight.shape[1]
    direct = devices == 16
    block = jnp.concatenate([frozen_key_weight, adapter_down_weight], axis=1)
    if direct:
        complete, returned_cot = gather_blocks(devices, block, cotangent)
    else:
        complete = lax.all_gather(block, "dp", axis=0, tiled=True)
        returned_cot = lax.all_to_all(cotangent, "dp", split_axis=0, concat_axis=0, tiled=True)
    selector_rows = place_rows(plan, slot_count, per_peer).astype(jnp.bfloat16)
    tenant_picker = tenant_mask(tenant, feature_width)
    both = jnp.dot(tokens, complete, preferred_element_type=jnp.float32)
    latent_state = (both[:, features:] * tenant_picker).astype(jnp.bfloat16)
    key_output = (
        both[:, :features]
        + adapter_scale
        * jnp.dot(latent_state, adapter_up_weight, preferred_element_type=jnp.float32)
    ).astype(jnp.bfloat16)
    send_out = jnp.dot(selector_rows, key_output, preferred_element_type=jnp.float32).astype(
        jnp.bfloat16
    )
    row_gradient = leading_product(selector_rows, returned_cot).astype(jnp.bfloat16)
    mixing_factor = (
        adapter_scale * trailing_product(row_gradient, adapter_up_weight) * tenant_picker
    ).astype(jnp.bfloat16)
    token_gradient = trailing_product(
        jnp.concatenate([row_gradient, mixing_factor], axis=1), complete
    ).astype(jnp.bfloat16)
    scale = (tokens.shape[0] * devices) ** -0.5
    up_portion = adapter_scale * leading_product(latent_state, row_gradient)
    if direct:
        down_grad, up_weight_gradient, placed_out = finish(
            devices, scale, tokens, mixing_factor, up_portion, send_out
        )
    else:
        placed_out = lax.all_to_all(send_out, "dp", split_axis=0, concat_axis=0, tiled=True)
        down_part = leading_product(tokens, mixing_factor)
        down_grad = lax.psum_scatter(down_part, "dp", scatter_dimension=0, tiled=True) * scale
        up_weight_gradient = lax.psum(up_portion, "dp") * scale
    return (placed_out, token_gradient, down_grad, up_weight_gradient)


def solution(mesh):
    return jax.shard_map(
        shards,
        mesh=mesh,
        in_specs=(
            P(("groups", "dp"), None),
            P(("groups", "dp")),
            P(("groups", "dp"), None),
            P("dp", None),
            P("dp", None),
            P(),
            P(("groups", "dp"), None),
        ),
        out_specs=(
            P(("groups", "dp"), None),
            P(("groups", "dp"), None),
            P(("groups", "dp"), None),
            P("groups", None),
        ),
        check_vma=False,
    )
```

```python
import functools

import jax
import jax.numpy as jnp
from jax import lax
from jax.experimental import pallas as pl
from jax.experimental.pallas import tpu as pltpu
from jax.sharding import PartitionSpec as P

ADAPTER_RANK = 16
SUBS = 2


adapter_scale = 2.0


def remote(src, dst, send_sem, recv_sem, target, axis="dp"):
    return pltpu.make_async_remote_copy(
        src_ref=src,
        dst_ref=dst,
        send_sem=send_sem,
        recv_sem=recv_sem,
        device_id={axis: target},
        device_id_type=pl.DeviceIdType.MESH,
    )


def greet_all(me, devices, twin=None):
    barrier = pltpu.get_barrier_semaphore()
    targets = [{"dp": lax.rem(me + offset, devices)} for offset in range(1, devices)]
    if twin is not None:
        targets.append({"groups": twin})
    for target in targets:
        pl.semaphore_signal(
            barrier, inc=1, device_id=target, device_id_type=pl.DeviceIdType.MESH
        )
    pl.semaphore_wait(barrier, len(targets))


def ring_position(chip, around):
    z, y = chip // 2, chip % 2
    return z + y * (around - 1 - 2 * z)


def ring_chip(position, around):
    back = position // (around // 2)
    return 2 * position + back * (2 * around - 1 - 4 * position)


def gather_kernel(
    devices, block_ref, cot_ref, full_ref, rows_ref,
    own_sem, own_cot_sem, ring_send, ring_recv, side_send, side_recv,
    own_side_send, own_side_recv, cot_send, cot_recv,
    twin_send, twin_recv, twin_side_send, twin_side_recv,
):
    me = lax.axis_index("dp")
    around = devices // 2
    chip, core = me // 2, me % 2
    sibling = chip * 2 + 1 - core
    spot = ring_position(chip, around)
    depth = block_ref.shape[0]
    group = lax.axis_index("groups")
    single = depth * 5 // 32
    double = depth // 2 - 2 * single
    slots = cot_ref.shape[0] // devices

    def chip_at(hops):
        return ring_chip(lax.rem(spot + hops + around, around), around)

    def rows_of(way, sub, holder):
        if sub == 0:
            return holder * (depth - 2 * single) + way * single, single
        return 2 * single + way * double, double

    def piece_of(device, way, sub, holder):
        first, count = rows_of(way, sub, holder)
        return full_ref.at[pl.ds(device * depth + first, count)]

    own = pltpu.make_async_copy(block_ref, full_ref.at[pl.ds(me * depth, depth)], own_sem)
    own.start()
    own_cot = pltpu.make_async_copy(
        cot_ref.at[pl.ds(me * slots, slots)], rows_ref.at[pl.ds(me * slots, slots)], own_cot_sem
    )
    own_cot.start()
    greet_all(me, devices, 1 - group)
    pending = []

    ways = (1, -1)
    for sub in range(SUBS):
        for way in range(2):
            first, count = rows_of(way, sub, group)
            copy = remote(
                block_ref.at[pl.ds(first, count)], piece_of(me, way, sub, group), ring_send.at[way, sub, 0],
                ring_recv.at[way, sub, 0], chip_at(ways[way]) * 2 + core,
            )
            copy.start()
            pending.append(copy)
    side = remote(
        block_ref, full_ref.at[pl.ds(me * depth, depth)], own_side_send, own_side_recv, sibling
    )
    side.start()
    cots = []
    for offset in range(1, devices):
        peer = lax.rem(me + offset, devices)
        copy = remote(
            cot_ref.at[pl.ds(peer * slots, slots)], rows_ref.at[pl.ds(me * slots, slots)],
            cot_send.at[offset], cot_recv.at[offset], peer,
        )
        copy.start()
        cots.append(copy)

    sides = []

    def relay_twin(step):
        for way in range(2):
            origin = chip_at(-ways[way] * (step + 1))
            here = piece_of(origin * 2 + core, way, 0, 1 - group)
            remote(
                here, here, twin_send.at[way, step], twin_recv.at[way, step], 1 - group, "groups"
            ).wait_recv()
            sems = twin_side_send.at[way, step], twin_side_recv.at[way, step]
            copy = remote(here, here, *sems, sibling)
            copy.start()
            sides.append((copy, piece_of(origin * 2 + 1 - core, way, 0, 1 - group), *sems))

    for step in range(around - 1):
        for sub in range(SUBS):
            for way in range(2):
                origin = chip_at(-ways[way] * (step + 1))
                here = piece_of(origin * 2 + core, way, sub, group)
                remote(
                    here, here, ring_send.at[way, sub, step], ring_recv.at[way, sub, step], sibling
                ).wait_recv()
                if step < around - 2:
                    copy = remote(
                        here, here, ring_send.at[way, sub, step + 1],
                        ring_recv.at[way, sub, step + 1], chip_at(ways[way]) * 2 + core,
                    )
                    copy.start()
                    pending.append(copy)
                if sub == 0:
                    copy = remote(
                        here, here, twin_send.at[way, step], twin_recv.at[way, step],
                        1 - group, "groups",
                    )
                    copy.start()
                    pending.append(copy)
                sems = side_send.at[way, sub, step], side_recv.at[way, sub, step]
                copy = remote(here, here, *sems, sibling)
                copy.start()
                sides.append((copy, piece_of(origin * 2 + 1 - core, way, sub, group), *sems))
        if step > 0:
            relay_twin(step - 1)
    relay_twin(around - 2)

    own.wait()
    own_cot.wait()
    for offset in range(1, devices):
        cots[offset - 1].wait_send()
        origin = lax.rem(me - offset + devices, devices)
        place = rows_ref.at[pl.ds(origin * slots, slots)]
        remote(place, place, cot_send.at[offset], cot_recv.at[offset], sibling).wait_recv()
    for copy in pending:
        copy.wait_send()
    side.wait_send()
    place = full_ref.at[pl.ds(sibling * depth, depth)]
    remote(place, place, own_side_send, own_side_recv, sibling).wait_recv()
    for copy, place, send_sem, recv_sem in sides:
        copy.wait_send()
        remote(place, place, send_sem, recv_sem, sibling).wait_recv()


def gather_blocks(devices, block, cotangent):
    dma = pltpu.SemaphoreType.DMA
    steps = devices // 2 - 1
    anywhere = pl.BlockSpec(memory_space=pl.ANY)
    return pl.pallas_call(
        functools.partial(gather_kernel, devices),
        out_shape=(
            jax.ShapeDtypeStruct((devices * block.shape[0], block.shape[1]), block.dtype),
            jax.ShapeDtypeStruct(cotangent.shape, cotangent.dtype),
        ),
        in_specs=[anywhere] * 2,
        out_specs=(anywhere, anywhere),
        scratch_shapes=[
            dma, dma,
            dma((2, SUBS, steps)), dma((2, SUBS, steps)),
            dma((2, SUBS, steps)), dma((2, SUBS, steps)),
            dma, dma,
            dma((devices,)), dma((devices,)),
            dma((2, steps)), dma((2, steps)),
            dma((2, steps)), dma((2, steps)),
        ],
        compiler_params=pltpu.CompilerParams(
            collective_id=0, has_side_effects=True, vmem_limit_bytes=48 * 1024 * 1024
        ),
    )(block, cotangent)


def finish_kernel(
    devices, scale, tokens_ref, mix_ref, up_ref, send_ref, down_out, up_out, placed_ref,
    part_buf, side_buf, y_buf, y_land, z_buf, z_land, up_side, up_buf, up_land,
    own_sem, place_send, place_recv, side_send, side_recv, y_send, y_recv, z_send, z_recv,
    up_side_send, up_side_recv, up_send, up_recv, share_send, share_recv, last_send, last_recv,
):
    me = lax.axis_index("dp")
    chips, deep = devices // 2, devices // 4
    chip, core = me // 2, me % 2
    z, y = chip // 2, chip % 2
    sibling = chip * 2 + 1 - core
    across = (z * 2 + 1 - y) * 2 + core
    slots = send_ref.shape[0] // devices
    depth = down_out.shape[0]
    order = list(range(1, deep)) + [0]

    def device_of(hop, row, parity):
        return (lax.rem(z + hop, deep) * 2 + row) * 2 + parity

    def part(device):
        columns = pl.ds(pl.multiple_of(device * depth, depth), depth)
        return leading_product(tokens_ref[:, columns], mix_ref[...])

    own = pltpu.make_async_copy(
        send_ref.at[pl.ds(me * slots, slots)], placed_ref.at[pl.ds(me * slots, slots)], own_sem
    )
    own.start()
    greet_all(me, devices)

    up_pair = remote(up_ref.at[:, 1 - core], up_side, up_side_send, up_side_recv, sibling)
    up_pair.start()
    up_pair.wait()
    ups = []
    for offset in range(1, chips):
        target = lax.rem(chip + offset, chips)
        up_buf[offset] = up_ref[target, core] + up_side[target]
        copy = remote(
            up_buf.at[offset], up_land.at[offset], up_send.at[offset], up_recv.at[offset],
            target * 2 + core,
        )
        copy.start()
        ups.append(copy)

    places = []
    for offset in range(1, devices):
        peer = lax.rem(me + offset, devices)
        copy = remote(
            send_ref.at[pl.ds(peer * slots, slots)], placed_ref.at[pl.ds(me * slots, slots)],
            place_send.at[offset], place_recv.at[offset], peer,
        )
        copy.start()
        places.append(copy)

    sides = []
    for row in range(2):
        for hop in order:
            slot = row * deep + hop
            part_buf[slot] = part(device_of(hop, 1 - y if row == 0 else y, 1 - core))
            copy = remote(
                part_buf.at[slot], side_buf.at[slot], side_send.at[slot], side_recv.at[slot],
                sibling,
            )
            copy.start()
            sides.append(copy)
        if row == 0:
            over = []
            for hop in order:
                mine = part(device_of(hop, 1 - y, core))
                sides[len(over)].wait()
                y_buf[hop] = (mine + side_buf[hop]).astype(jnp.bfloat16)
                copy = remote(y_buf.at[hop], y_land.at[hop], y_send.at[hop], y_recv.at[hop], across)
                copy.start()
                over.append(copy)

    along = []
    for count, hop in enumerate(order):
        mine = part(device_of(hop, y, core))
        sides[deep + count].wait()
        mine = mine + side_buf[deep + hop]
        over[count].wait()
        mine = mine + y_land[hop].astype(jnp.float32)
        if hop == 0:
            down_out[...] = mine
        else:
            z_buf[hop] = mine.astype(jnp.bfloat16)
            copy = remote(
                z_buf.at[hop], z_land.at[hop], z_send.at[hop], z_recv.at[hop],
                device_of(hop, y, core),
            )
            copy.start()
            along.append(copy)

    total = up_ref[chip, core] + up_side[chip]
    for offset in range(1, chips):
        ups[offset - 1].wait()
        total = total + up_land[offset]
    up_out[chip, core] = total * scale
    shares = []
    for offset in range(1, chips):
        target = lax.rem(chip + offset, chips)
        copy = remote(
            up_out.at[chip, core], up_out.at[chip, core],
            share_send.at[offset], share_recv.at[offset], target * 2 + core,
        )
        copy.start()
        shares.append(copy)
    for offset in range(1, chips):
        shares[offset - 1].wait_send()
        place = up_out.at[lax.rem(chip - offset + chips, chips), core]
        remote(place, place, share_send.at[offset], share_recv.at[offset], sibling).wait_recv()
    mine_up, other_up = up_out.at[:, core], up_out.at[:, 1 - core]
    last = remote(mine_up, mine_up, last_send, last_recv, sibling)
    last.start()

    for copy in along:
        copy.wait()
    total = down_out[...]
    for hop in range(1, deep):
        total = total + z_land[hop].astype(jnp.float32)
    down_out[...] = total * scale

    own.wait()
    for offset in range(1, devices):
        origin = lax.rem(me - offset + devices, devices)
        places[offset - 1].wait_send()
        place = placed_ref.at[pl.ds(origin * slots, slots)]
        remote(place, place, place_send.at[offset], place_recv.at[offset], sibling).wait_recv()
    last.wait_send()
    remote(other_up, other_up, last_send, last_recv, sibling).wait_recv()


def finish(devices, scale, tokens, mixing_factor, up_portion, send_out):
    dma = pltpu.SemaphoreType.DMA
    chips, deep = devices // 2, devices // 4
    depth, width = tokens.shape[1] // devices, mixing_factor.shape[1]
    share, features = up_portion.shape[0] // devices, up_portion.shape[1]
    anywhere = pl.BlockSpec(memory_space=pl.ANY)
    local = pl.BlockSpec(memory_space=pltpu.VMEM)
    up_shape = (chips, 2, share, features)
    down, up, placed = pl.pallas_call(
        functools.partial(finish_kernel, devices, scale),
        out_shape=(
            jax.ShapeDtypeStruct((depth, width), jnp.float32),
            jax.ShapeDtypeStruct(up_shape, jnp.float32),
            jax.ShapeDtypeStruct(send_out.shape, send_out.dtype),
        ),
        in_specs=[local, local, local, anywhere],
        out_specs=(local, local, anywhere),
        scratch_shapes=[
            pltpu.VMEM((chips, depth, width), jnp.float32),
            pltpu.VMEM((chips, depth, width), jnp.float32),
            pltpu.VMEM((deep, depth, width), jnp.bfloat16),
            pltpu.VMEM((deep, depth, width), jnp.bfloat16),
            pltpu.VMEM((deep, depth, width), jnp.bfloat16),
            pltpu.VMEM((deep, depth, width), jnp.bfloat16),
            pltpu.VMEM((chips, share, features), jnp.float32),
            pltpu.VMEM((chips, share, features), jnp.float32),
            pltpu.VMEM((chips, share, features), jnp.float32),
            dma,
            dma((devices,)), dma((devices,)),
            dma((chips,)), dma((chips,)),
            dma((deep,)), dma((deep,)),
            dma((deep,)), dma((deep,)),
            dma, dma,
            dma((chips,)), dma((chips,)),
            dma((chips,)), dma((chips,)),
            dma, dma,
        ],
        compiler_params=pltpu.CompilerParams(
            collective_id=1, has_side_effects=True, vmem_limit_bytes=48 * 1024 * 1024
        ),
    )(tokens, mixing_factor, up_portion.reshape(up_shape), send_out)
    return down, up.reshape(up_portion.shape), placed


def place_rows(plan, slot_count, per_peer):
    destination = plan[:, 0]
    position = jnp.arange(destination.shape[0], dtype=jnp.int32)
    earlier_rows = (destination[None, :] == destination[:, None]) & (
        position[None, :] < position[:, None]
    )
    target_slot = destination * per_peer + jnp.sum(earlier_rows.astype(jnp.int32), axis=1)
    return (jnp.arange(slot_count, dtype=jnp.int32)[:, None] == target_slot[None, :]).astype(
        jnp.int32
    )


def tenant_mask(owners, feature_width):
    columns = jnp.arange(feature_width, dtype=jnp.int32) // ADAPTER_RANK
    return (columns[None, :] == owners[:, None]).astype(jnp.float32)


def leading_product(left, right):
    return lax.dot_general(
        left, right, (((0,), (0,)), ((), ())), preferred_element_type=jnp.float32
    )


def trailing_product(left, right):
    return lax.dot_general(
        left, right, (((1,), (1,)), ((), ())), preferred_element_type=jnp.float32
    )


def shards(
    tokens, tenant, plan, frozen_key_weight, adapter_down_weight, adapter_up_weight, cotangent
):
    devices = lax.axis_size("dp")
    slot_count = cotangent.shape[0]
    per_peer = slot_count // devices
    features = frozen_key_weight.shape[1]
    feature_width = adapter_down_weight.shape[1]
    direct = devices == 16
    block = jnp.concatenate([frozen_key_weight, adapter_down_weight], axis=1)
    if direct:
        complete, returned_cot = gather_blocks(devices, block, cotangent)
    else:
        complete = lax.all_gather(block, "dp", axis=0, tiled=True)
        returned_cot = lax.all_to_all(cotangent, "dp", split_axis=0, concat_axis=0, tiled=True)
    selector_rows = place_rows(plan, slot_count, per_peer).astype(jnp.bfloat16)
    tenant_picker = tenant_mask(tenant, feature_width)
    both = jnp.dot(tokens, complete, preferred_element_type=jnp.float32)
    latent_state = (both[:, features:] * tenant_picker).astype(jnp.bfloat16)
    key_output = (
        both[:, :features]
        + adapter_scale
        * jnp.dot(latent_state, adapter_up_weight, preferred_element_type=jnp.float32)
    ).astype(jnp.bfloat16)
    send_out = jnp.dot(selector_rows, key_output, preferred_element_type=jnp.float32).astype(
        jnp.bfloat16
    )
    row_gradient = leading_product(selector_rows, returned_cot).astype(jnp.bfloat16)
    mixing_factor = (
        adapter_scale * trailing_product(row_gradient, adapter_up_weight) * tenant_picker
    ).astype(jnp.bfloat16)
    token_gradient = trailing_product(
        jnp.concatenate([row_gradient, mixing_factor], axis=1), complete
    ).astype(jnp.bfloat16)
    scale = (tokens.shape[0] * devices) ** -0.5
    up_portion = adapter_scale * leading_product(latent_state, row_gradient)
    if direct:
        down_grad, up_weight_gradient, placed_out = finish(
            devices, scale, tokens, mixing_factor, up_portion, send_out
        )
    else:
        placed_out = lax.all_to_all(send_out, "dp", split_axis=0, concat_axis=0, tiled=True)
        down_part = leading_product(tokens, mixing_factor)
        down_grad = lax.psum_scatter(down_part, "dp", scatter_dimension=0, tiled=True) * scale
        up_weight_gradient = lax.psum(up_portion, "dp") * scale
    return (placed_out, token_gradient, down_grad, up_weight_gradient)


def solution(mesh):
    return jax.shard_map(
        shards,
        mesh=mesh,
        in_specs=(
            P(("groups", "dp"), None),
            P(("groups", "dp")),
            P(("groups", "dp"), None),
            P("dp", None),
            P("dp", None),
            P(),
            P(("groups", "dp"), None),
        ),
        out_specs=(
            P(("groups", "dp"), None),
            P(("groups", "dp"), None),
            P(("groups", "dp"), None),
            P("groups", None),
        ),
        check_vma=False,
    )
```
